32 devices in a mesh: groups: 2 (over y), section: 16 (over z, x, core).
Axes of the slice: x: 2, y: 2, z: 4, core: 2. Of those that a mesh axis runs over, the one named last changes fastest.
Arguments:
- held: bfloat16 [16, 128, 4096], P('section', 'groups'), parts along dimension 1, may hold values from 0 to 2
- tile_values: bfloat16 [4608, 128, 128], P('section'), may hold values from -0.25 to 0.25
- tile_rows: int32 [4608], P('section'), may hold values from 0 to 255
- tile_cols: int32 [4608], P('section'), may hold values from 0 to 31
- tile_count: int32 [16], P('section'), may hold values from 1 to 288, as said below
- bias: float32 [65536], P('section'), may hold values from -0.5 to -0.2
Outputs:
- settled: bfloat16 [16, 128, 4096], P('section', 'groups'), parts along dimension 1
The draws below stay inside these ranges and needn't reach their ends.
There are 2 independent parts, one for each index of `groups`. The reference program is written for one: setup_inputs(seed, part) draws one part's arguments, and reference() takes and returns one part's arrays. A program takes and returns all parts, laid end to end along the dimension named above; an argument that names none is the same for every part. Nothing has to cross between parts.
Inputs may be any that keep to these rules, and one draw needn't show every extreme that they name: `tile_count`: slots at or after a list's count are ignored; in every draw some list has all 288 slots live. `tile_rows`: pairs of tile row and tile column may repeat within a list; repeated tiles add.
All inputs are finite; a program needn't handle non-finite values.
Results may differ from the reference program's by a relative error of at most 0.0053.
Values may be sent and summed in bfloat16 or wider, within the bound.
A program may use at most 64 MiB of HBM per device.

```python
import jax
import jax.numpy as jnp
from jax import lax

TILE = 128
NTILES = 256
SPLIT = 8
CAP = 288
TICKS = 2
BATCH = 64
NEURONS = 32768
SLAB = 4096
COLT = 32
LAYERS = 2


def draw_tile_count(key, part):
    total_lists = LAYERS * SPLIT
    key_first = jax.random.fold_in(key, 11)
    key_second = jax.random.fold_in(key, 23)
    bottom = max(1, CAP // 10)
    ceiling = CAP * 7 // 10 + 1
    counts = jax.random.randint(key_first, (total_lists,), bottom, ceiling, dtype=jnp.int32)
    chosen = jax.random.randint(key_second, (), 0, total_lists, dtype=jnp.int32)
    return jnp.where(jnp.arange(total_lists, dtype=jnp.int32) == chosen, CAP, counts).astype(jnp.int32)


def plant(values, rng, low, largest):
    index_at = [jax.random.randint(jax.random.fold_in(rng, axis), (), 0, length) for axis, length in enumerate(values.shape)]
    longest = values.shape.index(max(values.shape))
    next_to = index_at[:longest] + [(index_at[longest] + 1) % values.shape[longest]] + index_at[longest + 1:]
    return values.at[tuple(index_at)].set(low).at[tuple(next_to)].set(largest)


def block_scale(key, extent, split, low, high):
    def one(axis_at, parts):
        heights = jax.random.uniform(jax.random.fold_in(jax.random.fold_in(key, 6), axis_at), (parts,), jnp.float32, low / len(split), high / len(split))
        return jnp.repeat(jnp.exp(heights), extent[axis_at] // parts).reshape((-1,) + (1,) * (len(extent) - axis_at - 1))

    loudness = one(*split[0])
    for cut in split[1:]:
        loudness = loudness * one(*cut)
    return loudness


def gaussian(key, extent, spread, limit, cuts=(), kind=jnp.bfloat16):
    gain = block_scale(key, extent, cuts, -0.22, 0.18) if cuts else 1.0
    result = jax.random.normal(key, extent, jnp.float32) * spread * gain
    return jnp.minimum(jnp.maximum(result, -limit), limit).astype(kind)


def setup_inputs(seed: int = 0, part: int = 0) -> dict:
    key_list = jax.random.split(jax.random.key(seed), 7)
    part_keys = jax.random.split(jax.random.fold_in(key_list[6], part), 7)
    held = jnp.clip(2.0 * jax.random.uniform(part_keys[0], (LAYERS * SPLIT, BATCH, SLAB), jnp.float32) ** block_scale(part_keys[0], (LAYERS * SPLIT, BATCH, SLAB), ((0, 16),), -0.2, 0.2), 0.0, 2.0).astype(jnp.bfloat16)
    tile_values = gaussian(key_list[1], (LAYERS * SPLIT * CAP, TILE, TILE), (max(NTILES * TILE // 64, 4 * TILE)) ** -0.5, 0.25, ((0, 16),))
    tile_rows = plant(jax.random.randint(key_list[2], (LAYERS * SPLIT * CAP,), 0, NTILES), jax.random.fold_in(key_list[2], 1), 0, NTILES - 1).astype(jnp.int32)
    tile_cols = plant(jax.random.randint(key_list[3], (LAYERS * SPLIT * CAP,), 0, COLT), jax.random.fold_in(key_list[3], 1), 0, COLT - 1).astype(jnp.int32)
    tile_count = draw_tile_count(jax.random.fold_in(key_list[6], 71), part)
    bias = jnp.clip(-0.5 + 0.3 * jax.random.uniform(key_list[5], (LAYERS * NEURONS,), jnp.float32) ** block_scale(key_list[5], (LAYERS * NEURONS,), ((0, 16),), -0.2, 0.2), -0.5, -0.2)
    return dict(held=held, tile_values=tile_values, tile_rows=tile_rows, tile_cols=tile_cols, tile_count=tile_count, bias=bias)


def layer_slab(full_input, rows_list, cols_list, live_count, values_list, bias_slab):
    batch_rows = full_input.shape[0]
    blocks = full_input.reshape(batch_rows, NTILES, TILE)
    picked = jnp.take(blocks, rows_list, axis=1)
    products = jnp.einsum("bck,ckj->cbj", picked.astype(jnp.float32), values_list.astype(jnp.float32))
    live = jnp.arange(CAP, dtype=jnp.int32) < live_count
    masked = jnp.where(live[:, None, None], products, jnp.zeros_like(products))
    summed = jax.ops.segment_sum(masked, cols_list, num_segments=COLT)
    summed = summed.transpose(1, 0, 2).reshape(batch_rows, COLT * TILE)
    return jnp.maximum(summed + bias_slab[None, :], 0.0).astype(jnp.bfloat16)


def reference(held, tile_values, tile_rows, tile_cols, tile_count, bias):
    devices_all = LAYERS * SPLIT
    values_all = tile_values.reshape(devices_all, CAP, TILE, TILE)
    rows_all = tile_rows.reshape(devices_all, CAP)
    cols_all = tile_cols.reshape(devices_all, CAP)
    bias_all = bias.reshape(devices_all, SLAB)
    indices = jnp.arange(devices_all, dtype=jnp.int32)
    current = held
    outputs = held
    for tick_index in range(TICKS):
        inputs_all = current.reshape(LAYERS, SPLIT, BATCH, SLAB).transpose(0, 2, 1, 3).reshape(LAYERS, BATCH, NEURONS)

        def device_layer(packed):
            index, values_list, rows_list, cols_list, live_count, bias_slab = packed
            full_input = inputs_all[index // SPLIT]
            return layer_slab(full_input, rows_list, cols_list, live_count, values_list, bias_slab)

        outputs = lax.map(device_layer, (indices, values_all, rows_all, cols_all, tile_count, bias_all))
        if tick_index + 1 < TICKS:
            current = jnp.roll(outputs, SPLIT, axis=0)
    return outputs
```

```python
import functools

import jax
import jax.numpy as jnp
from jax import lax
from jax.experimental import pallas as pl
from jax.experimental.pallas import tpu as pltpu
from jax.sharding import PartitionSpec as P

TILE = 128
SPLIT = 8
COLT = 32
HALVES = 2
PIECES = 2
PIECE = COLT // PIECES
GROUP = 8
WPARTS = 4
SIB, XN, ZN = 1, 2, 4
N_SENDS = HALVES * (14 + 16)


def kernel(peers, rows_ref, prev_ref, last_ref, held_ref, w_hbm, bias_ref, out_ref,
           xa0, xa1, xb0, xb1, y0, y1, w, buf, wsem, send_sem, recv_sem):
    xs = ((xa0, xa1), (xb0, xb1))
    ys = (y0, y1)
    slots = rows_ref.shape[0]
    part = held_ref.shape[1] // HALVES
    me = lax.axis_index("section")
    place = me % SPLIT
    base = me - place
    bits = (place % 2, (place // 2) % 2, place // 4)
    nxt = (me + SPLIT) % peers
    prv = (me + peers - SPLIT) % peers

    def moved(rel):
        at = place
        for b in range(3):
            if rel >> b & 1:
                at = at + (1 - 2 * bits[b]) * (1 << b)
        return at

    def slab(x, rel, k):
        return x.at[pl.ds(moved(rel) * COLT + k * PIECE, PIECE)]

    wsize = slots // WPARTS
    wcopies = [
        pltpu.make_async_copy(
            w_hbm.at[pl.ds(i * wsize, wsize)], w.at[pl.ds(i * wsize, wsize)], wsem.at[i])
        for i in range(WPARTS)
    ]
    for c in wcopies:
        c.start()

    barrier = pltpu.get_barrier_semaphore()
    for dev in (base + moved(SIB), base + moved(XN), base + moved(ZN), nxt, prv):
        pl.semaphore_signal(barrier, inc=1, device_id={"section": dev},
                            device_id_type=pl.DeviceIdType.MESH)

    for h in range(HALVES):
        for c in range(COLT):
            xs[0][h][place * COLT + c] = held_ref[0, h * part:(h + 1) * part, c * TILE:(c + 1) * TILE]
    buf[slots] = jnp.zeros(buf.shape[1:], buf.dtype)
    pl.semaphore_wait(barrier, 5)

    sent = []

    def send(t, h, rel, k, hop):
        x = xs[t][h]
        copy = pltpu.make_async_remote_copy(
            src_ref=slab(x, rel, k), dst_ref=slab(x, rel, k),
            send_sem=send_sem.at[len(sent)], recv_sem=recv_sem.at[t, h, rel ^ hop, k],
            device_id={"section": base + moved(hop)}, device_id_type=pl.DeviceIdType.MESH)
        copy.start()
        sent.append(copy)

    def send_next(h, k):
        copy = pltpu.make_async_remote_copy(
            src_ref=ys[h].at[pl.ds(k * PIECE, PIECE)], dst_ref=slab(xs[1][h], 0, k),
            send_sem=send_sem.at[len(sent)], recv_sem=recv_sem.at[1, h, 0, k],
            device_id={"section": nxt}, device_id_type=pl.DeviceIdType.MESH)
        copy.start()
        sent.append(copy)

    def arrive(t, h, rel, k):
        x = xs[t][h]
        pltpu.make_async_remote_copy(
            src_ref=slab(x, rel, k), dst_ref=slab(x, rel, k),
            send_sem=send_sem.at[0], recv_sem=recv_sem.at[t, h, rel, k],
            device_id={"section": base + moved(SIB)},
            device_id_type=pl.DeviceIdType.MESH).wait_recv()

    def step(t, h, rel, k, hops):
        def run():
            arrive(t, h, rel, k)
            for hop in hops:
                send(t, h, rel, k, hop)
        return run

    def own(h):
        for k in range(PIECES):
            send(0, h, 0, k, ZN)
            send(0, h, 0, PIECES - 1 - k, XN)
        for k in range(PIECES):
            send(0, h, 0, k, SIB)

    def gather_steps(h):
        return [
            step(0, h, ZN, 0, (XN, SIB)),
            step(0, h, XN, 1, (ZN, SIB)),
            step(0, h, ZN, 1, (SIB,)),
            step(0, h, XN, 0, (SIB,)),
            step(0, h, XN + ZN, 0, (SIB,)),
            step(0, h, XN + ZN, 1, (SIB,)),
        ]

    def pass_steps(h):
        every = []
        for rel, hops in ((0, (ZN, XN, SIB)), (ZN, (XN, SIB)), (XN, (SIB,)), (XN + ZN, (SIB,))):
            every += [step(1, h, rel, k, hops) for k in range(PIECES)]
        return every

    def settle(t, h):
        for rel in (1, 3, 5, 7):
            for k in range(PIECES):
                arrive(t, h, rel, k)

    def tiles(x, low, high):
        def body(i, carry):
            done = []
            for j in range(GROUP):
                s = i * GROUP + j
                done.append(jnp.dot(x[rows_ref[s]], w[s], preferred_element_type=jnp.float32))
            for j in range(GROUP):
                s = i * GROUP + j
                buf[s] = done[j] + buf[prev_ref[s]]
            return carry
        lax.fori_loop(low, high, body, 0)

    def layer(t, h, steps, segments, first):
        groups = slots // GROUP
        edges = [groups * i // segments for i in range(segments + 1)]
        steps = list(steps)
        for i in range(segments):
            tiles(xs[t][h], edges[i], edges[i + 1])
            if i >= first and steps:
                steps.pop(0)()
        for run in steps:
            run()
        for c in range(COLT):
            value = jnp.maximum(buf[last_ref[c]] + bias_ref[c:c + 1, :], 0.0).astype(jnp.bfloat16)
            if t == 0:
                ys[h][c] = value
                if (c + 1) % PIECE == 0:
                    send_next(h, c // PIECE)
            else:
                out_ref[0, h * part:(h + 1) * part, c * TILE:(c + 1) * TILE] = value

    own(0)
    early = gather_steps(0)
    for run in early[:2]:
        run()
    own(1)
    for run in early[2:]:
        run()
    settle(0, 0)
    for c in wcopies:
        c.wait()
    layer(0, 0, gather_steps(1), 7, 0)
    settle(0, 1)
    first_pass = pass_steps(0)
    layer(0, 1, first_pass[:1], 4, 2)
    for run in first_pass[1:]:
        run()
    settle(1, 0)
    layer(1, 0, pass_steps(1), 9, 0)
    settle(1, 1)
    layer(1, 1, (), 1, 0)
    for copy in sent:
        copy.wait_send()


def links(cols, live_count):
    slots = cols.shape[0]
    at = jnp.arange(slots, dtype=jnp.int32)
    same = (cols[:, None] == cols[None, :]) & (at[None, :] < at[:, None])
    prev = jnp.max(jnp.where(same, at[None, :], -1), axis=1)
    mine = (cols[None, :] == jnp.arange(COLT, dtype=jnp.int32)[:, None]) & (at < live_count)[None, :]
    last = jnp.max(jnp.where(mine, at[None, :], -1), axis=1)
    return jnp.where(prev < 0, slots, prev), jnp.where(last < 0, slots, last)


def on_device(peers, held, tile_values, tile_rows, tile_cols, tile_count, bias):
    slots = tile_rows.shape[0]
    batch = held.shape[1]
    part = batch // HALVES
    prev, last = links(tile_cols, tile_count[0])
    smem = pl.BlockSpec(memory_space=pltpu.SMEM)
    vmem = pl.BlockSpec(memory_space=pltpu.VMEM)
    x = pltpu.VMEM((SPLIT * COLT, part, TILE), jnp.bfloat16)
    y = pltpu.VMEM((COLT, part, TILE), jnp.bfloat16)
    return pl.pallas_call(
        functools.partial(kernel, peers),
        out_shape=jax.ShapeDtypeStruct(held.shape, jnp.bfloat16),
        in_specs=[smem, smem, smem, vmem, pl.BlockSpec(memory_space=pl.ANY), vmem],
        out_specs=vmem,
        scratch_shapes=[
            x, x, x, x, y, y,
            pltpu.VMEM((slots, TILE, TILE), jnp.bfloat16),
            pltpu.VMEM((slots + 1, part, TILE), jnp.float32),
            pltpu.SemaphoreType.DMA((WPARTS,)),
            pltpu.SemaphoreType.DMA((N_SENDS,)),
            pltpu.SemaphoreType.DMA((2, HALVES, SPLIT, PIECES)),
        ],
        compiler_params=pltpu.CompilerParams(
            collective_id=0, has_side_effects=True, vmem_limit_bytes=56 * 1024 * 1024),
    )(tile_rows, prev, last, held, tile_values, bias.reshape(COLT, TILE))


def solution(mesh):
    return jax.shard_map(
        functools.partial(on_device, mesh.shape["section"]),
        mesh=mesh,
        in_specs=(
            P("section", "groups", None),
            P("section", None, None),
            P("section"),
            P("section"),
            P("section"),
            P("section"),
        ),
        out_specs=P("section", "groups", None),
        check_vma=False,
    )
```

```python
import functools

import jax
import jax.numpy as jnp
from jax import lax
from jax.experimental import pallas as pl
from jax.experimental.pallas import tpu as pltpu
from jax.sharding import PartitionSpec as P

TILE = 128
SPLIT = 8
COLT = 32
HALVES = 2
PIECES = 2
PIECE = COLT // PIECES
GROUP = 40
LANES = 384
WPARTS = 4
SIB, XN, ZN = 1, 2, 4
N_SENDS = HALVES * (14 + 16)


def order(rows, cols, count):
    slots = cols.shape[1]
    pairs = (slots + COLT) // 2

    def iota(shape, axis):
        return lax.broadcasted_iota(jnp.int32, shape, axis)

    def total(mask, value, axis):
        return jnp.sum(jnp.where(mask, value, 0), axis=axis, keepdims=True)

    square = (slots, slots)
    diagonal = iota(square, 0) == iota(square, 1)

    def upright(line):
        return total(diagonal, line, 1)

    key = jnp.where(iota((1, slots), 1) < count, cols, COLT)
    key_up = upright(key)
    rank = total((key_up == key) & (iota(square, 0) < iota(square, 1)), 1, 0)
    below = total(key_up < key, 1, 0)
    column_up = iota((COLT, slots), 0)
    held_by = total(column_up == key, 1, 1)
    odd = held_by & 1
    pads = total(column_up < key, odd, 0)
    position = jnp.where(key < COLT, below + pads + rank, -1)

    wide = (slots, LANES)
    here = upright(position) == iota(wide, 1)
    zero_row = SPLIT * COLT
    slot = total(here, iota(wide, 0), 0)
    row = zero_row + total(here, upright(rows) - zero_row, 0)
    opens = total(here & (upright(rank) == 0), 1, 0)

    column = iota((COLT, LANES), 1)
    column_up = iota((COLT, LANES), 0)
    upto = total(column_up <= column, held_by + odd, 0)
    mine = total(column_up == column, held_by, 0)
    closes = jnp.where(mine > 0, (upto >> 1) - 1, pairs)
    slot = jnp.clip(slot, 0, slots - 1)
    row = jnp.clip(row, 0, zero_row)
    closes = jnp.clip(closes, 0, pairs)
    return jnp.concatenate([slot, row, opens, closes, jnp.zeros((4, LANES), jnp.int32)], axis=0)


def kernel(peers, count_ref, rows_ref, cols_ref, held_ref, w_hbm, bias_ref, out_ref,
           xa0, xa1, xb0, xb1, y0, y1, w, buf, plan, plan_ref, wsem, psem, send_sem, recv_sem):
    xs = ((xa0, xa1), (xb0, xb1))
    ys = (y0, y1)
    slots = rows_ref.shape[1]
    pairs = (slots + COLT) // 2
    part = held_ref.shape[1] // HALVES
    me = lax.axis_index("section")
    place = me % SPLIT
    base = me - place
    bits = (place % 2, (place // 2) % 2, place // 4)
    nxt = (me + SPLIT) % peers
    prv = (me + peers - SPLIT) % peers

    def moved(rel):
        at = place
        for b in range(3):
            if rel >> b & 1:
                at = at + (1 - 2 * bits[b]) * (1 << b)
        return at

    def slab(x, rel, k):
        return x.at[pl.ds(moved(rel) * COLT + k * PIECE, PIECE)]

    wsize = slots // WPARTS
    wcopies = [
        pltpu.make_async_copy(
            w_hbm.at[pl.ds(i * wsize, wsize)], w.at[pl.ds(i * wsize, wsize)], wsem.at[i])
        for i in range(WPARTS)
    ]
    for c in wcopies:
        c.start()

    barrier = pltpu.get_barrier_semaphore()
    for dev in (base + moved(SIB), base + moved(XN), base + moved(ZN), nxt, prv):
        pl.semaphore_signal(barrier, inc=1, device_id={"section": dev},
                            device_id_type=pl.DeviceIdType.MESH)

    for h in range(HALVES):
        for c in range(COLT):
            xs[0][h][place * COLT + c] = held_ref[0, h * part:(h + 1) * part, c * TILE:(c + 1) * TILE]
    buf[pairs] = jnp.zeros(buf.shape[1:], buf.dtype)
    for x in xs[0] + xs[1]:
        x[SPLIT * COLT] = jnp.zeros(x.shape[1:], x.dtype)
    pl.semaphore_wait(barrier, 5)

    sent = []

    def send(t, h, rel, k, hop):
        x = xs[t][h]
        copy = pltpu.make_async_remote_copy(
            src_ref=slab(x, rel, k), dst_ref=slab(x, rel, k),
            send_sem=send_sem.at[len(sent)], recv_sem=recv_sem.at[t, h, rel ^ hop, k],
            device_id={"section": base + moved(hop)}, device_id_type=pl.DeviceIdType.MESH)
        copy.start()
        sent.append(copy)

    def send_next(h, k):
        copy = pltpu.make_async_remote_copy(
            src_ref=ys[h].at[pl.ds(k * PIECE, PIECE)], dst_ref=slab(xs[1][h], 0, k),
            send_sem=send_sem.at[len(sent)], recv_sem=recv_sem.at[1, h, 0, k],
            device_id={"section": nxt}, device_id_type=pl.DeviceIdType.MESH)
        copy.start()
        sent.append(copy)

    def arrive(t, h, rel, k):
        x = xs[t][h]
        pltpu.make_async_remote_copy(
            src_ref=slab(x, rel, k), dst_ref=slab(x, rel, k),
            send_sem=send_sem.at[0], recv_sem=recv_sem.at[t, h, rel, k],
            device_id={"section": base + moved(SIB)},
            device_id_type=pl.DeviceIdType.MESH).wait_recv()

    def step(t, h, rel, k, hops):
        def run():
            arrive(t, h, rel, k)
            for hop in hops:
                send(t, h, rel, k, hop)
        return run

    def own(h):
        for k in range(PIECES):
            send(0, h, 0, k, ZN)
            send(0, h, 0, PIECES - 1 - k, XN)
        for k in range(PIECES):
            send(0, h, 0, k, SIB)

    def gather_steps(h):
        return [
            step(0, h, ZN, 0, (XN, SIB)),
            step(0, h, XN, 1, (ZN, SIB)),
            step(0, h, ZN, 1, (SIB,)),
            step(0, h, XN, 0, (SIB,)),
            step(0, h, XN + ZN, 0, (SIB,)),
            step(0, h, XN + ZN, 1, (SIB,)),
        ]

    def pass_steps(h):
        every = []
        for rel, hops in ((0, (ZN, XN, SIB)), (ZN, (XN, SIB)), (XN, (SIB,)), (XN + ZN, (SIB,))):
            every += [step(1, h, rel, k, hops) for k in range(PIECES)]
        return every

    def settle(t, h):
        for rel in (1, 3, 5, 7):
            for k in range(PIECES):
                arrive(t, h, rel, k)

    def tiles(x, low, high, total):
        def body(i, total):
            for j in range(GROUP):
                pair = i * GROUP + j
                a, b = 2 * pair, 2 * pair + 1
                left = jnp.concatenate([x[plan_ref[1, a]], x[plan_ref[1, b]]], axis=1)
                right = jnp.concatenate([w[plan_ref[0, a]], w[plan_ref[0, b]]], axis=0)
                product = jnp.dot(left, right, preferred_element_type=jnp.float32)
                total = jnp.where(plan_ref[2, a] == 1, product, total + product)
                buf[pair] = total
            return total
        return lax.fori_loop(low, high, body, total)

    def layer(t, h, steps, segments, first):
        groups = pairs // GROUP
        edges = [groups * i // segments for i in range(segments + 1)]
        steps = list(steps)
        each = -(-len(steps) // max(1, segments - first))
        total = jnp.zeros(buf.shape[1:], buf.dtype)
        for i in range(segments):
            total = tiles(xs[t][h], edges[i], edges[i + 1], total)
            if i >= first:
                for run in steps[:each]:
                    run()
                steps = steps[each:]
        for run in steps:
            run()
        for c in range(COLT):
            value = jnp.maximum(buf[plan_ref[3, c]] + bias_ref[c:c + 1, :], 0.0).astype(jnp.bfloat16)
            if t == 0:
                ys[h][c] = value
                if (c + 1) % PIECE == 0:
                    send_next(h, c // PIECE)
            else:
                out_ref[0, h * part:(h + 1) * part, c * TILE:(c + 1) * TILE] = value

    own(0)
    plan[...] = order(rows_ref[...], cols_ref[...], count_ref[0])
    plan_copy = pltpu.make_async_copy(plan, plan_ref, psem)
    plan_copy.start()
    early = gather_steps(0)
    for run in early[:2]:
        run()
    own(1)
    for run in early[2:]:
        run()
    settle(0, 0)
    plan_copy.wait()
    for c in wcopies:
        c.wait()
    layer(0, 0, gather_steps(1), 4, 0)
    settle(0, 1)
    first_pass = pass_steps(0)
    layer(0, 1, first_pass[:1], 4, 2)
    for run in first_pass[1:]:
        run()
    settle(1, 0)
    layer(1, 0, pass_steps(1), 4, 0)
    settle(1, 1)
    layer(1, 1, (), 1, 0)
    for copy in sent:
        copy.wait_send()


def on_device(peers, held, tile_values, tile_rows, tile_cols, tile_count, bias):
    slots = tile_rows.shape[0]
    batch = held.shape[1]
    part = batch // HALVES
    pairs = (slots + COLT) // 2
    smem = pl.BlockSpec(memory_space=pltpu.SMEM)
    vmem = pl.BlockSpec(memory_space=pltpu.VMEM)
    x = pltpu.VMEM((SPLIT * COLT + 1, part, TILE), jnp.bfloat16)
    y = pltpu.VMEM((COLT, part, TILE), jnp.bfloat16)
    return pl.pallas_call(
        functools.partial(kernel, peers),
        out_shape=jax.ShapeDtypeStruct(held.shape, jnp.bfloat16),
        in_specs=[smem, vmem, vmem, vmem, pl.BlockSpec(memory_space=pl.ANY), vmem],
        out_specs=vmem,
        scratch_shapes=[
            x, x, x, x, y, y,
            pltpu.VMEM((slots, TILE, TILE), jnp.bfloat16),
            pltpu.VMEM((pairs + 1, part, TILE), jnp.float32),
            pltpu.VMEM((8, LANES), jnp.int32),
            pltpu.SMEM((8, LANES), jnp.int32),
            pltpu.SemaphoreType.DMA((WPARTS,)),
            pltpu.SemaphoreType.DMA,
            pltpu.SemaphoreType.DMA((N_SENDS,)),
            pltpu.SemaphoreType.DMA((2, HALVES, SPLIT, PIECES)),
        ],
        compiler_params=pltpu.CompilerParams(
            collective_id=0, has_side_effects=True, vmem_limit_bytes=56 * 1024 * 1024),
    )(tile_count, tile_rows.reshape(1, slots), tile_cols.reshape(1, slots), held, tile_values, bias.reshape(COLT, TILE))


def solution(mesh):
    return jax.shard_map(
        functools.partial(on_device, mesh.shape["section"]),
        mesh=mesh,
        in_specs=(
            P("section", "groups", None),
            P("section", None, None),
            P("section"),
            P("section"),
            P("section"),
            P("section"),
        ),
        out_specs=P("section", "groups", None),
        check_vma=False,
    )
```

```python
import functools

import jax
import jax.numpy as jnp
from jax import lax
from jax.experimental import pallas as pl
from jax.experimental.pallas import tpu as pltpu
from jax.sharding import PartitionSpec as P

TILE = 128
SPLIT = 8
COLT = 32
HALVES = 2
PIECES = 2
PIECE = COLT // PIECES
GROUP = 40
LANES = 384
WPARTS = 4
SIB, XN, ZN = 1, 2, 4
N_SENDS = HALVES * PIECES * (7 + 8)


def order(rows, cols, count):
    slots = cols.shape[1]
    pairs = (slots + COLT) // 2

    def iota(shape, axis):
        return lax.broadcasted_iota(jnp.int32, shape, axis)

    def total(mask, value, axis):
        return jnp.sum(jnp.where(mask, value, 0), axis=axis, keepdims=True)

    square = (slots, slots)
    diagonal = iota(square, 0) == iota(square, 1)

    def upright(line):
        return total(diagonal, line, 1)

    key = jnp.where(iota((1, slots), 1) < count, cols, COLT)
    key_up = upright(key)
    rank = total((key_up == key) & (iota(square, 0) < iota(square, 1)), 1, 0)
    below = total(key_up < key, 1, 0)
    column_up = iota((COLT, slots), 0)
    held_by = total(column_up == key, 1, 1)
    odd = held_by & 1
    pads = total(column_up < key, odd, 0)
    position = jnp.where(key < COLT, below + pads + rank, -1)

    wide = (slots, LANES)
    here = upright(position) == iota(wide, 1)
    zero_row = SPLIT * COLT
    slot = total(here, iota(wide, 0), 0)
    row = zero_row + total(here, upright(rows) - zero_row, 0)
    opens = total(here & (upright(rank) == 0), 1, 0)

    column = iota((COLT, LANES), 1)
    column_up = iota((COLT, LANES), 0)
    upto = total(column_up <= column, held_by + odd, 0)
    mine = total(column_up == column, held_by, 0)
    closes = jnp.where(mine > 0, (upto >> 1) - 1, pairs)
    slot = jnp.clip(slot, 0, slots - 1)
    row = jnp.clip(row, 0, zero_row)
    closes = jnp.clip(closes, 0, pairs)
    return jnp.concatenate([slot, row, opens, closes, jnp.zeros((4, LANES), jnp.int32)], axis=0)


def kernel(peers, count_ref, rows_ref, cols_ref, held_ref, w_hbm, bias_ref, out_ref,
           xa0, xa1, xb0, xb1, y0, y1, w, buf, plan, plan_ref, wsem, psem, send_sem, recv_sem):
    xs = ((xa0, xa1), (xb0, xb1))
    ys = (y0, y1)
    slots = rows_ref.shape[0]
    pairs = (slots + COLT) // 2
    part = held_ref.shape[1] // HALVES
    me = lax.axis_index("section")
    place = me % SPLIT
    base = me - place
    bits = (place % 2, (place // 2) % 2, place // 4)
    nxt = (me + SPLIT) % peers
    prv = (me + peers - SPLIT) % peers

    def moved(rel):
        at = place
        for b in range(3):
            if rel >> b & 1:
                at = at + (1 - 2 * bits[b]) * (1 << b)
        return at

    def slab(x, rel, k):
        return x.at[pl.ds(moved(rel) * COLT + k * PIECE, PIECE)]

    wsize = slots // WPARTS
    wcopies = [
        pltpu.make_async_copy(
            w_hbm.at[pl.ds(i * wsize, wsize)], w.at[pl.ds(i * wsize, wsize)], wsem.at[i])
        for i in range(WPARTS)
    ]
    for c in wcopies:
        c.start()

    barrier = pltpu.get_barrier_semaphore()
    for dev in (base + moved(SIB), base + moved(XN), base + moved(ZN), nxt, prv):
        pl.semaphore_signal(barrier, inc=1, device_id={"section": dev},
                            device_id_type=pl.DeviceIdType.MESH)

    for h in range(HALVES):
        for c in range(COLT):
            xs[0][h][place * COLT + c] = held_ref[0, h * part:(h + 1) * part, c * TILE:(c + 1) * TILE]
    buf[pairs] = jnp.zeros(buf.shape[1:], buf.dtype)
    for x in xs[0] + xs[1]:
        x[SPLIT * COLT] = jnp.zeros(x.shape[1:], x.dtype)
    pl.semaphore_wait(barrier, 5)

    sent = []

    def send(t, h, rel, k, hop):
        x = xs[t][h]
        copy = pltpu.make_async_remote_copy(
            src_ref=slab(x, rel, k), dst_ref=slab(x, rel, k),
            send_sem=send_sem.at[len(sent)], recv_sem=recv_sem.at[t, h, rel ^ hop, k],
            device_id={"section": base + moved(hop)}, device_id_type=pl.DeviceIdType.MESH)
        copy.start()
        sent.append(copy)

    def send_next(h, k):
        copy = pltpu.make_async_remote_copy(
            src_ref=ys[h].at[pl.ds(k * PIECE, PIECE)], dst_ref=slab(xs[1][h], 0, k),
            send_sem=send_sem.at[len(sent)], recv_sem=recv_sem.at[1, h, 0, k],
            device_id={"section": nxt}, device_id_type=pl.DeviceIdType.MESH)
        copy.start()
        sent.append(copy)

    def arrive(t, h, rel, k):
        x = xs[t][h]
        pltpu.make_async_remote_copy(
            src_ref=slab(x, rel, k), dst_ref=slab(x, rel, k),
            send_sem=send_sem.at[0], recv_sem=recv_sem.at[t, h, rel, k],
            device_id={"section": base + moved(SIB)},
            device_id_type=pl.DeviceIdType.MESH).wait_recv()

    def step(t, h, rel, k, hops):
        def run():
            arrive(t, h, rel, k)
            for hop in hops:
                send(t, h, rel, k, hop)
        return run

    def own(h):
        for k in range(PIECES):
            send(0, h, 0, k, ZN)
            send(0, h, 0, (k + PIECES // 2) % PIECES, XN)
        for k in range(PIECES):
            send(0, h, 0, k, SIB)

    def gather_steps(h):
        direct, diagonal = [], []
        for i in range(PIECES):
            j = (i + PIECES // 2) % PIECES
            direct.append(step(0, h, ZN, i, (XN, SIB) if i < PIECES // 2 else (SIB,)))
            direct.append(step(0, h, XN, j, (ZN, SIB) if j >= PIECES // 2 else (SIB,)))
        for i in range(PIECES // 2):
            diagonal.append(step(0, h, XN + ZN, i, (SIB,)))
            diagonal.append(step(0, h, XN + ZN, i + PIECES // 2, (SIB,)))
        return direct + diagonal

    def pass_steps(h):
        every = []
        for k in range(PIECES):
            for rel, hops in ((0, (ZN, XN, SIB)), (ZN, (XN, SIB)), (XN, (SIB,)), (XN + ZN, (SIB,))):
                every.append(step(1, h, rel, k, hops))
        return every

    def settle(t, h):
        for rel in (1, 3, 5, 7):
            for k in range(PIECES):
                arrive(t, h, rel, k)

    def tiles(x, low, high, total):
        def body(i, total):
            for j in range(GROUP):
                pair = i * GROUP + j
                a, b = 2 * pair, 2 * pair + 1
                left = jnp.concatenate([x[plan_ref[1, a]], x[plan_ref[1, b]]], axis=1)
                right = jnp.concatenate([w[plan_ref[0, a]], w[plan_ref[0, b]]], axis=0)
                product = jnp.dot(left, right, preferred_element_type=jnp.float32)
                total = jnp.where(plan_ref[2, a] == 1, product, total + product)
                buf[pair] = total
            return total
        return lax.fori_loop(low, high, body, total)

    def layer(t, h, between):
        total = jnp.zeros(buf.shape[1:], buf.dtype)
        for i in range(pairs // GROUP):
            total = tiles(xs[t][h], i, i + 1, total)
            for run in between.get(i, ()):
                run()
        for c in range(COLT):
            value = jnp.maximum(buf[plan_ref[3, c]] + bias_ref[c:c + 1, :], 0.0).astype(jnp.bfloat16)
            if t == 0:
                ys[h][c] = value
                if (c + 1) % PIECE == 0:
                    send_next(h, c // PIECE)
            else:
                out_ref[0, h * part:(h + 1) * part, c * TILE:(c + 1) * TILE] = value

    own(0)
    plan[...] = order(rows_ref[...][None, :], cols_ref[...][None, :], count_ref[0])
    plan_copy = pltpu.make_async_copy(plan, plan_ref, psem)
    plan_copy.start()
    ahead = PIECES
    first = gather_steps(0)
    for run in first[:ahead]:
        run()
    own(1)
    for run in first[ahead:]:
        run()
    settle(0, 0)
    plan_copy.wait()
    for c in wcopies:
        c.wait()
    second = gather_steps(1)
    half = ahead // 2
    layer(0, 0, {1: second[:half], 2: second[half:ahead]})
    for run in second[ahead:]:
        run()
    settle(0, 1)
    layer(0, 1, {})
    for run in pass_steps(0):
        run()
    settle(1, 0)
    final = pass_steps(1)
    layer(1, 0, {i: final[i:i + 1] for i in range(4)})
    for run in final[4:]:
        run()
    settle(1, 1)
    layer(1, 1, {})
    for copy in sent:
        copy.wait_send()


def on_device(peers, held, tile_values, tile_rows, tile_cols, tile_count, bias):
    slots = tile_rows.shape[0]
    batch = held.shape[1]
    part = batch // HALVES
    pairs = (slots + COLT) // 2
    smem = pl.BlockSpec(memory_space=pltpu.SMEM)
    vmem = pl.BlockSpec(memory_space=pltpu.VMEM)
    x = pltpu.VMEM((SPLIT * COLT + 1, part, TILE), jnp.bfloat16)
    y = pltpu.VMEM((COLT, part, TILE), jnp.bfloat16)
    return pl.pallas_call(
        functools.partial(kernel, peers),
        out_shape=jax.ShapeDtypeStruct(held.shape, jnp.bfloat16),
        in_specs=[smem, vmem, vmem, vmem, pl.BlockSpec(memory_space=pl.ANY), vmem],
        out_specs=vmem,
        scratch_shapes=[
            x, x, x, x, y, y,
            pltpu.VMEM((slots, TILE, TILE), jnp.bfloat16),
            pltpu.VMEM((pairs + 1, part, TILE), jnp.float32),
            pltpu.VMEM((8, LANES), jnp.int32),
            pltpu.SMEM((8, LANES), jnp.int32),
            pltpu.SemaphoreType.DMA((WPARTS,)),
            pltpu.SemaphoreType.DMA,
            pltpu.SemaphoreType.DMA((N_SENDS,)),
            pltpu.SemaphoreType.DMA((2, HALVES, SPLIT, PIECES)),
        ],
        compiler_params=pltpu.CompilerParams(
            collective_id=0, has_side_effects=True, vmem_limit_bytes=56 * 1024 * 1024),
    )(tile_count, tile_rows, tile_cols, held, tile_values, bias.reshape(COLT, TILE))


def solution(mesh):
    return jax.shard_map(
        functools.partial(on_device, mesh.shape["section"]),
        mesh=mesh,
        in_specs=(
            P("section", "groups", None),
            P("section", None, None),
            P("section"),
            P("section"),
            P("section"),
            P("section"),
        ),
        out_specs=P("section", "groups", None),
        check_vma=False,
    )
```

```python
import functools

import jax
import jax.numpy as jnp
from jax import lax
from jax.experimental import pallas as pl
from jax.experimental.pallas import tpu as pltpu
from jax.sharding import PartitionSpec as P

TILE = 128
SPLIT = 8
COLT = 32
HALVES = 2
PIECES = 2
PIECE = COLT // PIECES
GROUP = 40
LANES = 384
WPARTS = 4
SIB, XN, ZN = 1, 2, 4
N_SENDS = HALVES * PIECES * (7 + 8)


def order(rows, cols, count):
    slots = cols.shape[1]
    pairs = (slots + COLT) // 2

    def iota(shape, axis):
        return lax.broadcasted_iota(jnp.int32, shape, axis)

    def total(mask, value, axis):
        return jnp.sum(jnp.where(mask, value, 0), axis=axis, keepdims=True)

    square = (slots, slots)
    diagonal = iota(square, 0) == iota(square, 1)

    def upright(line):
        return total(diagonal, line, 1)

    key = jnp.where(iota((1, slots), 1) < count, cols, COLT)
    key_up = upright(key)
    rank = total((key_up == key) & (iota(square, 0) < iota(square, 1)), 1, 0)
    below = total(key_up < key, 1, 0)
    column_up = iota((COLT, slots), 0)
    held_by = total(column_up == key, 1, 1)
    odd = held_by & 1
    pads = total(column_up < key, odd, 0)
    position = jnp.where(key < COLT, below + pads + rank, -1)

    wide = (slots, LANES)
    here = upright(position) == iota(wide, 1)
    zero_row = SPLIT * COLT
    slot = total(here, iota(wide, 0), 0)
    row = zero_row + total(here, upright(rows) - zero_row, 0)
    opens = total(here & (upright(rank) == 0), 1, 0)

    column = iota((COLT, LANES), 1)
    column_up = iota((COLT, LANES), 0)
    upto = total(column_up <= column, held_by + odd, 0)
    mine = total(column_up == column, held_by, 0)
    closes = jnp.where(mine > 0, (upto >> 1) - 1, pairs)
    slot = jnp.clip(slot, 0, slots - 1)
    row = jnp.clip(row, 0, zero_row)
    closes = jnp.clip(closes, 0, pairs)
    return jnp.concatenate([slot, row, opens, closes, jnp.zeros((4, LANES), jnp.int32)], axis=0)


def kernel(peers, count_ref, rows_ref, cols_ref, held_ref, w_hbm, bias_ref, out_ref,
           xa0, xa1, xb0, xb1, y0, y1, w, buf, plan, plan_ref, wsem, psem, send_sem, recv_sem):
    xs = ((xa0, xa1), (xb0, xb1))
    ys = (y0, y1)
    slots = rows_ref.shape[0]
    pairs = (slots + COLT) // 2
    part = held_ref.shape[1] // HALVES
    me = lax.axis_index("section")
    place = me % SPLIT
    base = me - place
    bits = (place % 2, (place // 2) % 2, place // 4)
    nxt = (me + SPLIT) % peers
    prv = (me + peers - SPLIT) % peers

    def moved(rel):
        at = place
        for b in range(3):
            if rel >> b & 1:
                at = at + (1 - 2 * bits[b]) * (1 << b)
        return at

    def slab(x, rel, k):
        return x.at[pl.ds(moved(rel) * COLT + k * PIECE, PIECE)]

    wsize = slots // WPARTS
    wcopies = [
        pltpu.make_async_copy(
            w_hbm.at[pl.ds(i * wsize, wsize)], w.at[pl.ds(i * wsize, wsize)], wsem.at[i])
        for i in range(WPARTS)
    ]
    for c in wcopies:
        c.start()

    barrier = pltpu.get_barrier_semaphore()
    for dev in (base + moved(SIB), base + moved(XN), base + moved(ZN), nxt, prv):
        pl.semaphore_signal(barrier, inc=1, device_id={"section": dev},
                            device_id_type=pl.DeviceIdType.MESH)

    for h in range(HALVES):
        for c in range(COLT):
            xs[0][h][place * COLT + c] = held_ref[0, h * part:(h + 1) * part, c * TILE:(c + 1) * TILE]
    buf[pairs] = jnp.zeros(buf.shape[1:], buf.dtype)
    for x in xs[0] + xs[1]:
        x[SPLIT * COLT] = jnp.zeros(x.shape[1:], x.dtype)
    pl.semaphore_wait(barrier, 5)

    sent, pushed = [], []

    def send(t, h, rel, k, hop):
        x = xs[t][h]
        copy = pltpu.make_async_remote_copy(
            src_ref=slab(x, rel, k), dst_ref=slab(x, rel, k),
            send_sem=send_sem.at[len(sent)], recv_sem=recv_sem.at[t, h, rel ^ hop, k],
            device_id={"section": base + moved(hop)}, device_id_type=pl.DeviceIdType.MESH)
        copy.start()
        sent.append(copy)

    def send_next(h, k):
        copy = pltpu.make_async_remote_copy(
            src_ref=ys[h].at[pl.ds(k * PIECE, PIECE)], dst_ref=slab(xs[1][h], 0, k),
            send_sem=send_sem.at[len(sent)], recv_sem=recv_sem.at[1, h, 0, k],
            device_id={"section": nxt}, device_id_type=pl.DeviceIdType.MESH)
        copy.start()
        sent.append(copy)
        pushed.append(copy)

    def push(h, k):
        if pushed:
            pushed[-1].wait_send()
        send_next(h, k)

    def arrive(t, h, rel, k):
        x = xs[t][h]
        pltpu.make_async_remote_copy(
            src_ref=slab(x, rel, k), dst_ref=slab(x, rel, k),
            send_sem=send_sem.at[0], recv_sem=recv_sem.at[t, h, rel, k],
            device_id={"section": base + moved(SIB)},
            device_id_type=pl.DeviceIdType.MESH).wait_recv()

    def step(t, h, rel, k, hops):
        def run():
            arrive(t, h, rel, k)
            for hop in hops:
                send(t, h, rel, k, hop)
        return run

    def own(h):
        for k in range(PIECES):
            send(0, h, 0, k, ZN)
            send(0, h, 0, (k + PIECES // 2) % PIECES, XN)
        for k in range(PIECES):
            send(0, h, 0, k, SIB)

    def gather_steps(h):
        direct, diagonal = [], []
        for i in range(PIECES):
            j = (i + PIECES // 2) % PIECES
            direct.append(step(0, h, ZN, i, (XN, SIB) if i < PIECES // 2 else (SIB,)))
            direct.append(step(0, h, XN, j, (ZN, SIB) if j >= PIECES // 2 else (SIB,)))
        for i in range(PIECES // 2):
            diagonal.append(step(0, h, XN + ZN, i, (SIB,)))
            diagonal.append(step(0, h, XN + ZN, i + PIECES // 2, (SIB,)))
        return direct + diagonal

    def pass_step(h, rel, k):
        hops = {0: (ZN, XN, SIB), ZN: (XN, SIB)}.get(rel, (SIB,))
        return step(1, h, rel, k, hops)

    def settle(t, h):
        for rel in (1, 3, 5, 7):
            for k in range(PIECES):
                arrive(t, h, rel, k)

    def tiles(x, low, high, total):
        def body(i, total):
            for j in range(GROUP):
                pair = i * GROUP + j
                a, b = 2 * pair, 2 * pair + 1
                left = jnp.concatenate([x[plan_ref[1, a]], x[plan_ref[1, b]]], axis=1)
                right = jnp.concatenate([w[plan_ref[0, a]], w[plan_ref[0, b]]], axis=0)
                product = jnp.dot(left, right, preferred_element_type=jnp.float32)
                total = jnp.where(plan_ref[2, a] == 1, product, total + product)
                buf[pair] = total
            return total
        return lax.fori_loop(low, high, body, total)

    def layer(t, h, between):
        total = jnp.zeros(buf.shape[1:], buf.dtype)
        for i in range(pairs // GROUP):
            total = tiles(xs[t][h], i, i + 1, total)
            for run in between.get(i, ()):
                run()
        for c in range(COLT):
            value = jnp.maximum(buf[plan_ref[3, c]] + bias_ref[c:c + 1, :], 0.0).astype(jnp.bfloat16)
            if t == 0:
                ys[h][c] = value
            else:
                out_ref[0, h * part:(h + 1) * part, c * TILE:(c + 1) * TILE] = value

    own(0)
    plan[...] = order(rows_ref[...][None, :], cols_ref[...][None, :], count_ref[0])
    plan_copy = pltpu.make_async_copy(plan, plan_ref, psem)
    plan_copy.start()
    for run in gather_steps(0):
        run()
    own(1)
    settle(0, 0)
    plan_copy.wait()
    for c in wcopies:
        c.wait()
    layer(0, 0, {})
    push(0, 0)
    for run in gather_steps(1):
        run()
    push(0, 1)
    settle(0, 1)
    pass_step(0, 0, 0)()
    layer(0, 1, {2: [pass_step(0, ZN, 0)]})
    push(1, 0)
    for rel, k in ((0, 1), (XN, 0), (XN + ZN, 0), (ZN, 1), (XN, 1)):
        pass_step(0, rel, k)()
    push(1, 1)
    pass_step(1, 0, 0)()
    pass_step(0, XN + ZN, 1)()
    settle(1, 0)
    layer(1, 0, {1: [pass_step(1, ZN, 0)]})
    for rel, k in ((XN, 0), (0, 1), (XN + ZN, 0), (ZN, 1), (XN, 1), (XN + ZN, 1)):
        pass_step(1, rel, k)()
    settle(1, 1)
    layer(1, 1, {})
    for copy in sent:
        if not any(copy is c for c in pushed[:-1]):
            copy.wait_send()


def on_device(peers, held, tile_values, tile_rows, tile_cols, tile_count, bias):
    slots = tile_rows.shape[0]
    batch = held.shape[1]
    part = batch // HALVES
    pairs = (slots + COLT) // 2
    smem = pl.BlockSpec(memory_space=pltpu.SMEM)
    vmem = pl.BlockSpec(memory_space=pltpu.VMEM)
    x = pltpu.VMEM((SPLIT * COLT + 1, part, TILE), jnp.bfloat16)
    y = pltpu.VMEM((COLT, part, TILE), jnp.bfloat16)
    return pl.pallas_call(
        functools.partial(kernel, peers),
        out_shape=jax.ShapeDtypeStruct(held.shape, jnp.bfloat16),
        in_specs=[smem, vmem, vmem, vmem, pl.BlockSpec(memory_space=pl.ANY), vmem],
        out_specs=vmem,
        scratch_shapes=[
            x, x, x, x, y, y,
            pltpu.VMEM((slots, TILE, TILE), jnp.bfloat16),
            pltpu.VMEM((pairs + 1, part, TILE), jnp.float32),
            pltpu.VMEM((8, LANES), jnp.int32),
            pltpu.SMEM((8, LANES), jnp.int32),
            pltpu.SemaphoreType.DMA((WPARTS,)),
            pltpu.SemaphoreType.DMA,
            pltpu.SemaphoreType.DMA((N_SENDS,)),
            pltpu.SemaphoreType.DMA((2, HALVES, SPLIT, PIECES)),
        ],
        compiler_params=pltpu.CompilerParams(
            collective_id=0, has_side_effects=True, vmem_limit_bytes=56 * 1024 * 1024),
    )(tile_count, tile_rows, tile_cols, held, tile_values, bias.reshape(COLT, TILE))


def solution(mesh):
    return jax.shard_map(
        functools.partial(on_device, mesh.shape["section"]),
        mesh=mesh,
        in_specs=(
            P("section", "groups", None),
            P("section", None, None),
            P("section"),
            P("section"),
            P("section"),
            P("section"),
        ),
        out_specs=P("section", "groups", None),
        check_vma=False,
    )
```

```python
import functools

import jax
import jax.numpy as jnp
from jax import lax
from jax.experimental import pallas as pl
from jax.experimental.pallas import tpu as pltpu
from jax.sharding import PartitionSpec as P

TILE = 128
SPLIT = 8
COLT = 32
PARTS = 3
PIECES = 2
PIECE = COLT // PIECES
GROUP = 40
LANES = 384
WPARTS = 4
SIB, XN, ZN = 1, 2, 4
N_SENDS = PARTS * PIECES * (7 + 8)


def order(rows, cols, count):
    slots = cols.shape[1]
    pairs = (slots + COLT) // 2

    def iota(shape, axis):
        return lax.broadcasted_iota(jnp.int32, shape, axis)

    def total(mask, value, axis):
        return jnp.sum(jnp.where(mask, value, 0), axis=axis, keepdims=True)

    square = (slots, slots)
    diagonal = iota(square, 0) == iota(square, 1)

    def upright(line):
        return total(diagonal, line, 1)

    key = jnp.where(iota((1, slots), 1) < count, cols, COLT)
    key_up = upright(key)
    rank = total((key_up == key) & (iota(square, 0) < iota(square, 1)), 1, 0)
    below = total(key_up < key, 1, 0)
    column_up = iota((COLT, slots), 0)
    held_by = total(column_up == key, 1, 1)
    odd = held_by & 1
    pads = total(column_up < key, odd, 0)
    position = jnp.where(key < COLT, below + pads + rank, -1)

    wide = (slots, LANES)
    here = upright(position) == iota(wide, 1)
    zero_row = SPLIT * COLT
    slot = total(here, iota(wide, 0), 0)
    row = zero_row + total(here, upright(rows) - zero_row, 0)
    opens = total(here & (upright(rank) == 0), 1, 0)

    column = iota((COLT, LANES), 1)
    column_up = iota((COLT, LANES), 0)
    upto = total(column_up <= column, held_by + odd, 0)
    mine = total(column_up == column, held_by, 0)
    closes = jnp.where(mine > 0, (upto >> 1) - 1, pairs)
    slot = jnp.clip(slot, 0, slots - 1)
    row = jnp.clip(row, 0, zero_row)
    closes = jnp.clip(closes, 0, pairs)
    return jnp.concatenate([slot, row, opens, closes, jnp.zeros((4, LANES), jnp.int32)], axis=0)


def kernel(peers, count_ref, rows_ref, cols_ref, held_ref, w_hbm, bias_ref, out_ref,
           xa0, xa1, xa2, xb0, xb1, xb2, y0, y1, y2, w, buf, plan, plan_ref, wsem, psem, send_sem, recv_sem):
    xs = ((xa0, xa1, xa2), (xb0, xb1, xb2))
    ys = (y0, y1, y2)
    slots = rows_ref.shape[0]
    pairs = (slots + COLT) // 2
    batch = held_ref.shape[1]
    starts = (0, batch // 4, batch * 3 // 4, batch)
    me = lax.axis_index("section")
    place = me % SPLIT
    base = me - place
    bits = (place % 2, (place // 2) % 2, place // 4)
    nxt = (me + SPLIT) % peers
    prv = (me + peers - SPLIT) % peers

    def moved(rel):
        at = place
        for b in range(3):
            if rel >> b & 1:
                at = at + (1 - 2 * bits[b]) * (1 << b)
        return at

    def slab(x, rel, k):
        return x.at[pl.ds(moved(rel) * COLT + k * PIECE, PIECE)]

    wsize = slots // WPARTS
    wcopies = [
        pltpu.make_async_copy(
            w_hbm.at[pl.ds(i * wsize, wsize)], w.at[pl.ds(i * wsize, wsize)], wsem.at[i])
        for i in range(WPARTS)
    ]
    for c in wcopies:
        c.start()

    barrier = pltpu.get_barrier_semaphore()
    for dev in (base + moved(SIB), base + moved(XN), base + moved(ZN), nxt, prv):
        pl.semaphore_signal(barrier, inc=1, device_id={"section": dev},
                            device_id_type=pl.DeviceIdType.MESH)

    for h in range(PARTS):
        for c in range(COLT):
            xs[0][h][place * COLT + c] = held_ref[0, starts[h]:starts[h + 1], c * TILE:(c + 1) * TILE]
    buf[pairs] = jnp.zeros(buf.shape[1:], buf.dtype)
    for x in xs[0] + xs[1]:
        x[SPLIT * COLT] = jnp.zeros(x.shape[1:], x.dtype)
    pl.semaphore_wait(barrier, 5)

    sent, pushed = [], []

    def send(t, h, rel, k, hop):
        x = xs[t][h]
        copy = pltpu.make_async_remote_copy(
            src_ref=slab(x, rel, k), dst_ref=slab(x, rel, k),
            send_sem=send_sem.at[len(sent)], recv_sem=recv_sem.at[t, h, rel ^ hop, k],
            device_id={"section": base + moved(hop)}, device_id_type=pl.DeviceIdType.MESH)
        copy.start()
        sent.append(copy)

    def send_next(h, k):
        copy = pltpu.make_async_remote_copy(
            src_ref=ys[h].at[pl.ds(k * PIECE, PIECE)], dst_ref=slab(xs[1][h], 0, k),
            send_sem=send_sem.at[len(sent)], recv_sem=recv_sem.at[1, h, 0, k],
            device_id={"section": nxt}, device_id_type=pl.DeviceIdType.MESH)
        copy.start()
        sent.append(copy)
        pushed.append(copy)

    def push(h, k):
        if pushed:
            pushed[-1].wait_send()
        send_next(h, k)

    def arrive(t, h, rel, k):
        x = xs[t][h]
        pltpu.make_async_remote_copy(
            src_ref=slab(x, rel, k), dst_ref=slab(x, rel, k),
            send_sem=send_sem.at[0], recv_sem=recv_sem.at[t, h, rel, k],
            device_id={"section": base + moved(SIB)},
            device_id_type=pl.DeviceIdType.MESH).wait_recv()

    def step(t, h, rel, k, hops):
        def run():
            arrive(t, h, rel, k)
            for hop in hops:
                send(t, h, rel, k, hop)
        return run

    def own(h):
        for k in range(PIECES):
            send(0, h, 0, k, ZN)
            send(0, h, 0, (k + PIECES // 2) % PIECES, XN)
        for k in range(PIECES):
            send(0, h, 0, k, SIB)

    def gather_steps(h):
        direct, diagonal = [], []
        for i in range(PIECES):
            j = (i + PIECES // 2) % PIECES
            direct.append(step(0, h, ZN, i, (XN, SIB) if i < PIECES // 2 else (SIB,)))
            direct.append(step(0, h, XN, j, (ZN, SIB) if j >= PIECES // 2 else (SIB,)))
        for i in range(PIECES // 2):
            diagonal.append(step(0, h, XN + ZN, i, (SIB,)))
            diagonal.append(step(0, h, XN + ZN, i + PIECES // 2, (SIB,)))
        return direct + diagonal

    def pass_step(h, rel, k):
        hops = {0: (ZN, XN, SIB), ZN: (XN, SIB)}.get(rel, (SIB,))
        return step(1, h, rel, k, hops)

    def settle(t, h):
        for rel in (1, 3, 5, 7):
            for k in range(PIECES):
                arrive(t, h, rel, k)

    def tiles(inputs, i, total):
        rows = total.shape[0]

        def tile(at):
            return jnp.concatenate([x[at] for x in inputs], axis=0)

        for j in range(GROUP):
            pair = i * GROUP + j
            a, b = 2 * pair, 2 * pair + 1
            left = jnp.concatenate([tile(plan_ref[1, a]), tile(plan_ref[1, b])], axis=1)
            right = jnp.concatenate([w[plan_ref[0, a]], w[plan_ref[0, b]]], axis=0)
            product = jnp.dot(left, right, preferred_element_type=jnp.float32)
            total = jnp.where(plan_ref[2, a] == 1, product, total + product)
            buf[pair, :rows] = total
        return total

    def layer(inputs, put, between):
        rows = sum(x.shape[1] for x in inputs)
        total = jnp.zeros((rows, TILE), buf.dtype)
        for i in range(pairs // GROUP):
            total = tiles(inputs, i, total)
            for run in between.get(i, ()):
                run()
        for c in range(COLT):
            value = buf[plan_ref[3, c], :rows] + bias_ref[c:c + 1, :]
            put(c, jnp.maximum(value, 0.0).astype(jnp.bfloat16))

    def tick(h, between):
        def put(c, value):
            ys[h][c] = value
        layer(xs[0][h:h + 1], put, between)

    def put_out(c, value):
        out_ref[0, :, c * TILE:(c + 1) * TILE] = value

    own(0)
    plan[...] = order(rows_ref[...][None, :], cols_ref[...][None, :], count_ref[0])
    plan_copy = pltpu.make_async_copy(plan, plan_ref, psem)
    plan_copy.start()
    def run_all(steps):
        for run in steps:
            run()

    second, third = gather_steps(1), gather_steps(2)
    run_all(gather_steps(0))
    own(1)
    settle(0, 0)
    plan_copy.wait()
    for c in wcopies:
        c.wait()
    tick(0, {})
    push(0, 0)
    run_all(second[:4])
    push(0, 1)
    run_all(second[4:])
    own(2)
    settle(0, 1)
    pass_step(0, 0, 0)()
    pass_step(0, 0, 1)()
    tick(1, {1: third[:4], 2: [pass_step(0, ZN, 0), pass_step(0, ZN, 1)]})
    push(1, 0)
    run_all(third[4:])
    settle(0, 2)
    for rel, k in ((XN, 0), (XN, 1), (XN + ZN, 0), (XN + ZN, 1)):
        pass_step(0, rel, k)()
    tick(2, {2: [lambda: push(1, 1)], 3: [pass_step(1, 0, 0)]})
    pass_step(1, ZN, 0)()
    pass_step(1, XN, 0)()
    push(2, 0)
    for h, rel, k in ((1, XN + ZN, 0), (1, 0, 1)):
        pass_step(h, rel, k)()
    push(2, 1)
    for h, rel, k in ((2, 0, 0), (1, ZN, 1), (1, XN, 1), (2, ZN, 0), (2, XN, 0), (2, 0, 1), (1, XN + ZN, 1),
                      (2, ZN, 1), (2, XN + ZN, 0), (2, XN, 1), (2, XN + ZN, 1)):
        pass_step(h, rel, k)()
    for h in range(PARTS):
        settle(1, h)
    layer(xs[1], put_out, {})
    for copy in sent:
        if not any(copy is c for c in pushed[:-1]):
            copy.wait_send()


def on_device(peers, held, tile_values, tile_rows, tile_cols, tile_count, bias):
    slots = tile_rows.shape[0]
    batch = held.shape[1]
    sizes = (batch // 4, batch // 2, batch // 4)
    pairs = (slots + COLT) // 2
    smem = pl.BlockSpec(memory_space=pltpu.SMEM)
    vmem = pl.BlockSpec(memory_space=pltpu.VMEM)
    xs = [pltpu.VMEM((SPLIT * COLT + 1, size, TILE), jnp.bfloat16) for size in sizes]
    ys = [pltpu.VMEM((COLT, size, TILE), jnp.bfloat16) for size in sizes]
    return pl.pallas_call(
        functools.partial(kernel, peers),
        out_shape=jax.ShapeDtypeStruct(held.shape, jnp.bfloat16),
        in_specs=[smem, vmem, vmem, vmem, pl.BlockSpec(memory_space=pl.ANY), vmem],
        out_specs=vmem,
        scratch_shapes=[
            *xs, *xs, *ys,
            pltpu.VMEM((slots, TILE, TILE), jnp.bfloat16),
            pltpu.VMEM((pairs + 1, batch, TILE), jnp.float32),
            pltpu.VMEM((8, LANES), jnp.int32),
            pltpu.SMEM((8, LANES), jnp.int32),
            pltpu.SemaphoreType.DMA((WPARTS,)),
            pltpu.SemaphoreType.DMA,
            pltpu.SemaphoreType.DMA((N_SENDS,)),
            pltpu.SemaphoreType.DMA((2, PARTS, SPLIT, PIECES)),
        ],
        compiler_params=pltpu.CompilerParams(
            collective_id=0, has_side_effects=True, vmem_limit_bytes=56 * 1024 * 1024),
    )(tile_count, tile_rows, tile_cols, held, tile_values, bias.reshape(COLT, TILE))


def solution(mesh):
    return jax.shard_map(
        functools.partial(on_device, mesh.shape["section"]),
        mesh=mesh,
        in_specs=(
            P("section", "groups", None),
            P("section", None, None),
            P("section"),
            P("section"),
            P("section"),
            P("section"),
        ),
        out_specs=P("section", "groups", None),
        check_vma=False,
    )
```

```python
import functools

import jax
import jax.numpy as jnp
from jax import lax
from jax.experimental import pallas as pl
from jax.experimental.pallas import tpu as pltpu
from jax.sharding import PartitionSpec as P

TILE = 128
SPLIT = 8
COLT = 32
HALVES = 2
PIECES = 2
PIECE = COLT // PIECES
GROUP = 40
LANES = 384
WPARTS = 4
SIB, XN, ZN = 1, 2, 4
N_SENDS = HALVES * PIECES * (7 + 8)


def order(rows, cols, count):
    slots = cols.shape[1]
    pairs = (slots + COLT) // 2

    def iota(shape, axis):
        return lax.broadcasted_iota(jnp.int32, shape, axis)

    def total(mask, value, axis):
        return jnp.sum(jnp.where(mask, value, 0), axis=axis, keepdims=True)

    square = (slots, slots)
    diagonal = iota(square, 0) == iota(square, 1)

    def upright(line):
        return total(diagonal, line, 1)

    key = jnp.where(iota((1, slots), 1) < count, cols, COLT)
    key_up = upright(key)
    rank = total((key_up == key) & (iota(square, 0) < iota(square, 1)), 1, 0)
    below = total(key_up < key, 1, 0)
    column_up = iota((COLT, slots), 0)
    held_by = total(column_up == key, 1, 1)
    odd = held_by & 1
    pads = total(column_up < key, odd, 0)
    position = jnp.where(key < COLT, below + pads + rank, -1)

    wide = (slots, LANES)
    here = upright(position) == iota(wide, 1)
    zero_row = SPLIT * COLT
    slot = total(here, iota(wide, 0), 0)
    row = zero_row + total(here, upright(rows) - zero_row, 0)
    opens = total(here & (upright(rank) == 0), 1, 0)

    column = iota((COLT, LANES), 1)
    column_up = iota((COLT, LANES), 0)
    upto = total(column_up <= column, held_by + odd, 0)
    mine = total(column_up == column, held_by, 0)
    closes = jnp.where(mine > 0, (upto >> 1) - 1, pairs)
    slot = jnp.clip(slot, 0, slots - 1)
    row = jnp.clip(row, 0, zero_row)
    closes = jnp.clip(closes, 0, pairs)
    return jnp.concatenate([slot, row, opens, closes, jnp.zeros((4, LANES), jnp.int32)], axis=0)


def kernel(peers, count_ref, rows_ref, cols_ref, held_ref, w_hbm, bias_ref, out_ref,
           xa0, xa1, xb0, xb1, y0, y1, w, buf, plan, plan_ref, wsem, psem, send_sem, recv_sem):
    xs = ((xa0, xa1), (xb0, xb1))
    ys = (y0, y1)
    slots = rows_ref.shape[0]
    pairs = (slots + COLT) // 2
    part = held_ref.shape[1] // HALVES
    me = lax.axis_index("section")
    place = me % SPLIT
    base = me - place
    bits = (place % 2, (place // 2) % 2, place // 4)
    nxt = (me + SPLIT) % peers
    prv = (me + peers - SPLIT) % peers

    def moved(rel):
        at = place
        for b in range(3):
            if rel >> b & 1:
                at = at + (1 - 2 * bits[b]) * (1 << b)
        return at

    def slab(x, rel, k):
        return x.at[pl.ds(moved(rel) * COLT + k * PIECE, PIECE)]

    wsize = slots // WPARTS
    wcopies = [
        pltpu.make_async_copy(
            w_hbm.at[pl.ds(i * wsize, wsize)], w.at[pl.ds(i * wsize, wsize)], wsem.at[i])
        for i in range(WPARTS)
    ]
    for c in wcopies:
        c.start()

    barrier = pltpu.get_barrier_semaphore()
    for dev in (base + moved(SIB), base + moved(XN), base + moved(ZN), nxt, prv):
        pl.semaphore_signal(barrier, inc=1, device_id={"section": dev},
                            device_id_type=pl.DeviceIdType.MESH)

    for h in range(HALVES):
        for c in range(COLT):
            xs[0][h][place * COLT + c] = held_ref[0, h * part:(h + 1) * part, c * TILE:(c + 1) * TILE]
    buf[pairs] = jnp.zeros(buf.shape[1:], buf.dtype)
    for x in xs[0] + xs[1]:
        x[SPLIT * COLT] = jnp.zeros(x.shape[1:], x.dtype)
    pl.semaphore_wait(barrier, 5)

    sent, pushed = [], []

    def send(t, h, rel, k, hop):
        x = xs[t][h]
        copy = pltpu.make_async_remote_copy(
            src_ref=slab(x, rel, k), dst_ref=slab(x, rel, k),
            send_sem=send_sem.at[len(sent)], recv_sem=recv_sem.at[t, h, rel ^ hop, k],
            device_id={"section": base + moved(hop)}, device_id_type=pl.DeviceIdType.MESH)
        copy.start()
        sent.append(copy)

    def send_next(h, k):
        copy = pltpu.make_async_remote_copy(
            src_ref=ys[h].at[pl.ds(k * PIECE, PIECE)], dst_ref=slab(xs[1][h], 0, k),
            send_sem=send_sem.at[len(sent)], recv_sem=recv_sem.at[1, h, 0, k],
            device_id={"section": nxt}, device_id_type=pl.DeviceIdType.MESH)
        copy.start()
        sent.append(copy)
        pushed.append(copy)

    def push(h, k):
        if pushed:
            pushed[-1].wait_send()
        send_next(h, k)

    def arrive(t, h, rel, k):
        x = xs[t][h]
        pltpu.make_async_remote_copy(
            src_ref=slab(x, rel, k), dst_ref=slab(x, rel, k),
            send_sem=send_sem.at[0], recv_sem=recv_sem.at[t, h, rel, k],
            device_id={"section": base + moved(SIB)},
            device_id_type=pl.DeviceIdType.MESH).wait_recv()

    def step(t, h, rel, k, hops):
        def run():
            arrive(t, h, rel, k)
            for hop in hops:
                send(t, h, rel, k, hop)
        return run

    def own(h):
        for k in range(PIECES):
            send(0, h, 0, k, ZN)
            send(0, h, 0, (k + PIECES // 2) % PIECES, XN)
        for k in range(PIECES):
            send(0, h, 0, k, SIB)

    def gather_steps(h):
        direct, diagonal = [], []
        for i in range(PIECES):
            j = (i + PIECES // 2) % PIECES
            direct.append(step(0, h, ZN, i, (XN, SIB) if i < PIECES // 2 else (SIB,)))
            direct.append(step(0, h, XN, j, (ZN, SIB) if j >= PIECES // 2 else (SIB,)))
        for i in range(PIECES // 2):
            diagonal.append(step(0, h, XN + ZN, i, (SIB,)))
            diagonal.append(step(0, h, XN + ZN, i + PIECES // 2, (SIB,)))
        return direct + diagonal

    def pass_step(h, rel, k):
        hops = {0: (ZN, XN, SIB), ZN: (XN, SIB)}.get(rel, (SIB,))
        return step(1, h, rel, k, hops)

    def settle(t, h):
        for rel in (1, 3, 5, 7):
            for k in range(PIECES):
                arrive(t, h, rel, k)

    def tiles(x, low, high, total):
        def body(i, total):
            for j in range(GROUP):
                pair = i * GROUP + j
                a, b = 2 * pair, 2 * pair + 1
                left = jnp.concatenate([x[plan_ref[1, a]], x[plan_ref[1, b]]], axis=1)
                right = jnp.concatenate([w[plan_ref[0, a]], w[plan_ref[0, b]]], axis=0)
                product = jnp.dot(left, right, preferred_element_type=jnp.float32)
                total = jnp.where(plan_ref[2, a] == 1, product, total + product)
                buf[pair] = total
            return total
        return lax.fori_loop(low, high, body, total)

    def layer(t, h, between):
        total = jnp.zeros(buf.shape[1:], buf.dtype)
        for i in range(pairs // GROUP):
            total = tiles(xs[t][h], i, i + 1, total)
            for run in between.get(i, ()):
                run()
        for c in range(COLT):
            value = jnp.maximum(buf[plan_ref[3, c]] + bias_ref[c:c + 1, :], 0.0).astype(jnp.bfloat16)
            if t == 0:
                ys[h][c] = value
            else:
                out_ref[0, h * part:(h + 1) * part, c * TILE:(c + 1) * TILE] = value

    own(0)
    plan[...] = order(rows_ref[...][None, :], cols_ref[...][None, :], count_ref[0])
    plan_copy = pltpu.make_async_copy(plan, plan_ref, psem)
    plan_copy.start()
    for run in gather_steps(0):
        run()
    own(1)
    settle(0, 0)
    plan_copy.wait()
    for c in wcopies:
        c.wait()
    layer(0, 0, {})
    push(0, 0)
    for run in gather_steps(1):
        run()
    push(0, 1)
    settle(0, 1)
    pass_step(0, 0, 0)()
    layer(0, 1, {1: [pass_step(0, ZN, 0)], 3: [pass_step(0, 0, 1)]})
    push(1, 0)
    for rel, k in ((XN, 0), (XN + ZN, 0), (ZN, 1), (XN, 1)):
        pass_step(0, rel, k)()
    push(1, 1)
    pass_step(1, 0, 0)()
    pass_step(0, XN + ZN, 1)()
    settle(1, 0)
    layer(1, 0, {
        0: [pass_step(1, ZN, 0)],
        1: [pass_step(1, XN, 0), pass_step(1, 0, 1)],
        2: [pass_step(1, XN + ZN, 0), pass_step(1, ZN, 1)],
        3: [pass_step(1, XN, 1)],
    })
    pass_step(1, XN + ZN, 1)()
    settle(1, 1)
    layer(1, 1, {})
    for copy in sent:
        if not any(copy is c for c in pushed[:-1]):
            copy.wait_send()


def on_device(peers, held, tile_values, tile_rows, tile_cols, tile_count, bias):
    slots = tile_rows.shape[0]
    batch = held.shape[1]
    part = batch // HALVES
    pairs = (slots + COLT) // 2
    smem = pl.BlockSpec(memory_space=pltpu.SMEM)
    vmem = pl.BlockSpec(memory_space=pltpu.VMEM)
    x = pltpu.VMEM((SPLIT * COLT + 1, part, TILE), jnp.bfloat16)
    y = pltpu.VMEM((COLT, part, TILE), jnp.bfloat16)
    return pl.pallas_call(
        functools.partial(kernel, peers),
        out_shape=jax.ShapeDtypeStruct(held.shape, jnp.bfloat16),
        in_specs=[smem, vmem, vmem, vmem, pl.BlockSpec(memory_space=pl.ANY), vmem],
        out_specs=vmem,
        scratch_shapes=[
            x, x, x, x, y, y,
            pltpu.VMEM((slots, TILE, TILE), jnp.bfloat16),
            pltpu.VMEM((pairs + 1, part, TILE), jnp.float32),
            pltpu.VMEM((8, LANES), jnp.int32),
            pltpu.SMEM((8, LANES), jnp.int32),
            pltpu.SemaphoreType.DMA((WPARTS,)),
            pltpu.SemaphoreType.DMA,
            pltpu.SemaphoreType.DMA((N_SENDS,)),
            pltpu.SemaphoreType.DMA((2, HALVES, SPLIT, PIECES)),
        ],
        compiler_params=pltpu.CompilerParams(
            collective_id=0, has_side_effects=True, vmem_limit_bytes=56 * 1024 * 1024),
    )(tile_count, tile_rows, tile_cols, held, tile_values, bias.reshape(COLT, TILE))


def solution(mesh):
    return jax.shard_map(
        functools.partial(on_device, mesh.shape["section"]),
        mesh=mesh,
        in_specs=(
            P("section", "groups", None),
            P("section", None, None),
            P("section"),
            P("section"),
            P("section"),
            P("section"),
        ),
        out_specs=P("section", "groups", None),
        check_vma=False,
    )
```
